32 devices in a mesh: angle: 8 (over y, x, core), block: 4 (over z).
Axes of the slice: x: 2, y: 2, z: 4, core: 2. Of those that a mesh axis runs over, the one named last changes fastest.
Arguments:
- object_field: float32 [32, 2, 512, 512], P(None, None, 'block'), may hold values from -1.5 to 1.5
- shears: int32 [8, 32], P('angle'), may hold values from -16 to 16, as said below
- positions: int32 [8, 4, 2], P('angle', 'block'), may hold values from 0 to 511
- measured: bfloat16 [8, 4, 512, 512], P('angle', 'block'), may hold values from 0 to 2
- probe_field: float32 [2, 512, 512], replicated
- kappa_field: float32 [8, 512, 512], P('angle'), may hold values from 0.01 to 0.1
Outputs:
- updated_object: float32 [32, 2, 512, 512], P(None, None, 'block')
The draws below stay inside these ranges and needn't reach their ends.
Inputs may be any that keep to these rules, and one draw needn't show every extreme that they name: `shears`: each angle's row offset of each slice; the values -16 and 16 occur in every draw.
All inputs are finite; a program needn't handle non-finite values.
Results may differ from the reference program's by a relative error of at most 0.0003.
Values sent between devices are 32-bit elements; how exact they have to be, the bound alone decides.
A program may use at most 192 MiB of HBM per device.

```python
import math
import jax
import jax.numpy as jnp
from jax import lax

NX = 512
NY = 512
Z = 32
STEPS = 2
SH = 16
ANGLES = 8
FRAMES = 4


def draw_probe_field(key, part):
    coord_x = (jnp.arange(NX, dtype=jnp.float32) - NX / 2) / (NX / 4)
    coord_y = (jnp.arange(NY, dtype=jnp.float32) - NY / 2) / (NY / 4)
    envelope = 0.25 + jnp.exp(-0.5 * (coord_x[:, None] ** 2 + coord_y[None, :] ** 2))
    noise = jax.random.normal(key, (2, NX, NY), jnp.float32)
    return (1.2 * noise * envelope[None]).astype(jnp.float32)


def draw_shears(key, part):
    base_key, high_key, low_key = jax.random.split(key, 3)
    values = jax.random.randint(base_key, (ANGLES * Z,), -SH, SH + 1)
    high_index = jax.random.randint(high_key, (), 0, ANGLES * Z)
    low_index = (high_index + 1 + jax.random.randint(low_key, (), 0, ANGLES * Z - 1)) % (ANGLES * Z)
    values = values.at[high_index].set(SH).at[low_index].set(-SH)
    return values.reshape(ANGLES, Z).astype(jnp.int32)


def with_ends(drawn, stream_key, smallest, largest):
    spot = [jax.random.randint(jax.random.fold_in(stream_key, axis), (), 0, length) for axis, length in enumerate(drawn.shape)]
    longest = drawn.shape.index(max(drawn.shape))
    beside = spot[:longest] + [(spot[longest] + 1) % drawn.shape[longest]] + spot[longest + 1:]
    return drawn.at[tuple(spot)].set(smallest).at[tuple(beside)].set(largest)


def steps_of(stream_key, extent, cuts, low, largest):
    level, own = 1.0, jax.random.fold_in(stream_key, 6)
    for axis_at, blocks in cuts:
        draws = jnp.exp(jax.random.uniform(jax.random.fold_in(own, axis_at), (blocks,), jnp.float32, low / len(cuts), largest / len(cuts)))
        level = level * jnp.repeat(draws, extent[axis_at] // blocks).reshape([-1 if axis == axis_at else 1 for axis in range(len(extent))])
    return level


def scatter_about(own_key, extent, width, most, cuts=(), kind=jnp.bfloat16):
    gain = steps_of(own_key, extent, cuts, -0.22, 0.18) if cuts else 1.0
    values = jax.random.normal(own_key, extent, jnp.float32) * width * gain
    return jnp.minimum(jnp.maximum(values, -most), most).astype(kind)


def setup_inputs(seed: int = 0) -> dict:
    keys = jax.random.split(jax.random.key(seed), 7)
    return {
        "object_field": scatter_about(keys[0], (Z, 2, NX, NY), 0.25, 1.5, ((2, 4),), jnp.float32),
        "shears": draw_shears(jax.random.fold_in(keys[6], 71), 0),
        "positions": with_ends(jax.random.randint(keys[2], (ANGLES, FRAMES, 2), 0, NX), jax.random.fold_in(keys[2], 1), 0, NX - 1).astype(jnp.int32),
        "measured": jnp.clip(2.0 * jax.random.uniform(keys[3], (ANGLES, FRAMES, NX, NY), jnp.float32) ** steps_of(keys[3], (ANGLES, FRAMES, NX, NY), ((0, 8), (1, 4)), -0.2, 0.2), 0.0, 2.0).astype(jnp.bfloat16),
        "probe_field": draw_probe_field(jax.random.fold_in(keys[6], 71), 0),
        "kappa_field": jnp.clip(jnp.exp(math.log(0.1) - 2.3025851 * jax.random.uniform(keys[5], (ANGLES, NX, NY), jnp.float32) ** steps_of(keys[5], (ANGLES, NX, NY), ((0, 8),), -0.2, 0.2)), 0.01, 0.1),
    }


def laplace(field):
    return jnp.roll(field, 1, -2) + jnp.roll(field, -1, -2) + jnp.roll(field, 1, -1) + jnp.roll(field, -1, -1) - 4.0 * field

def frame_loss(projected, probe_field, kappa_row, offset, observed):
    window = jnp.roll(projected, (-offset[0], -offset[1]), axis=(1, 2))
    real_part = probe_field[0] * window[0] - probe_field[1] * window[1]
    imag_part = probe_field[0] * window[1] + probe_field[1] * window[0]
    for step in range(STEPS):
        real_part, imag_part = (real_part - kappa_row * laplace(imag_part), imag_part + kappa_row * laplace(real_part))
    misfit = real_part * real_part + imag_part * imag_part - observed.astype(jnp.float32)
    return 0.5 * jnp.sum(misfit * misfit)

def reference(object_field, shears, positions, measured, probe_field, kappa_field):
    intensity = probe_field[0] * probe_field[0] + probe_field[1] * probe_field[1]

    def per_angle(summed, inputs):
        shear_row, offsets, observed_all, kappa_row = inputs
        moved = jax.vmap(lambda slab, amount: jnp.roll(slab, -amount, axis=1))(object_field, shear_row)
        projected = lax.optimization_barrier(jnp.sum(moved, axis=0))

        def per_frame(totals, frame_in):
            offset, observed = frame_in
            grads = jax.grad(frame_loss)(projected, probe_field, kappa_row, offset, observed)
            weight = jnp.roll(intensity, (offset[0], offset[1]), axis=(0, 1))
            return (totals + jnp.concatenate([grads, weight[None]], 0), None)
        totals, _ = lax.scan(per_frame, jnp.zeros((3, NX, NY), jnp.float32), (offsets, observed_all))
        unsheared = jax.vmap(lambda amount: jnp.roll(totals, amount, axis=1))(shear_row)
        return (summed + unsheared, None)
    summed, _ = lax.scan(per_angle, jnp.zeros((Z, 3, NX, NY), jnp.float32), (shears, positions, measured, kappa_field))
    return object_field - summed[:, :2] / (summed[:, 2:3] + 1.0)
```

```python
import functools
import jax
import jax.numpy as jnp
from jax import lax
from jax.experimental import pallas as pl
from jax.experimental.pallas import tpu as pltpu
from jax.sharding import PartitionSpec as P

NX = 512
NY = 512
STEPS = 2
SH = 16
EDGE = 24
LANES = 128
VMEM = pltpu.CompilerParams(vmem_limit_bytes=56 * 1024 * 1024)


def project_kernel(shears, field, out, padded):
    depth, rows = field.shape[0], field.shape[2]
    z0 = pl.program_id(1) * depth

    @pl.when(pl.program_id(1) == 0)
    def _():
        out[...] = jnp.zeros_like(out)
        zeros = jnp.zeros((depth, 2, 2 * SH, LANES), jnp.float32)
        padded[:, :, : 2 * SH] = zeros
        padded[:, :, 2 * SH + rows :] = zeros

    padded[:, :, 2 * SH : 2 * SH + rows] = field[...]
    for c in range(2):
        total = out[c]
        for z in range(depth):
            total = total + padded[z, c, pl.ds(SH + shears[0, z0 + z], rows + 2 * SH), :]
        out[c] = total


def project(shears, field):
    slices, _, rows, width = field.shape
    depth = 8
    return pl.pallas_call(
        project_kernel,
        out_shape=jax.ShapeDtypeStruct((2, rows + 2 * SH, width), jnp.float32),
        grid=(width // LANES, slices // depth),
        in_specs=[
            pl.BlockSpec(memory_space=pltpu.SMEM),
            pl.BlockSpec((depth, 2, rows, LANES), lambda i, j: (j, 0, 0, i)),
        ],
        out_specs=pl.BlockSpec((2, rows + 2 * SH, LANES), lambda i, j: (0, 0, i)),
        scratch_shapes=[pltpu.VMEM((depth, 2, rows + 4 * SH, LANES), jnp.float32)],
        compiler_params=VMEM,
        name="project",
    )(shears, field)


def spread(buffer, value, top):
    for j in range(NY // LANES):
        buffer[j, top : top + value.shape[0], :] = value[:, j * LANES : (j + 1) * LANES]


def rows_from(buffer, start, extent):
    parts = [buffer[j, pl.ds(start, extent), :] for j in range(NY // LANES)]
    return jnp.concatenate(parts, axis=1)


def shift_kernel(strips, positions, observed, out, wrapped):
    rows = NX // strips
    extent = rows + 2 * EDGE
    for f in range(observed.shape[0]):
        spread(wrapped, observed[f].astype(jnp.float32), 0)
        wrapped[:, NX:] = wrapped[:, :extent]
        p, q = positions[f, 0], positions[f, 1]
        for d in range(strips):
            start = lax.rem(d * rows - EDGE - p + 2 * NX, NX)
            out[d, f] = pltpu.roll(rows_from(wrapped, start, extent), q, 1)


def shift_measured(strips, positions, observed):
    extent = NX // strips + 2 * EDGE
    frames = observed.shape[0]
    return pl.pallas_call(
        functools.partial(shift_kernel, strips),
        out_shape=jax.ShapeDtypeStruct((strips, frames, extent, NY), jnp.float32),
        in_specs=[
            pl.BlockSpec(memory_space=pltpu.SMEM),
            pl.BlockSpec(memory_space=pltpu.VMEM),
        ],
        out_specs=pl.BlockSpec(memory_space=pltpu.VMEM),
        scratch_shapes=[pltpu.VMEM((NY // LANES, NX + extent, LANES), jnp.float32)],
        compiler_params=VMEM,
        name="shift_measured",
    )(positions, observed)


def laplace(field):
    rows, columns = field.shape
    return (
        pltpu.roll(field, 1, 0)
        + pltpu.roll(field, rows - 1, 0)
        + pltpu.roll(field, 1, 1)
        + pltpu.roll(field, columns - 1, 1)
        - 4.0 * field
    )


def frames_kernel(strip, positions, partial, before, after, observed, probe, kappa, out, wrapped, window):
    extent = window.shape[1]
    rows = extent - 2 * EDGE
    rim = EDGE - SH
    tall = EDGE + SH
    for i, source in enumerate((probe.at[0], probe.at[1], kappa)):
        spread(wrapped.at[i], source[...], 0)
        spread(wrapped.at[i], source[:extent], NX)
    window[:, :rim] = jnp.zeros((2, rim, NY), jnp.float32)
    window[:, rim + rows + 2 * SH :] = jnp.zeros((2, rim, NY), jnp.float32)
    window[:, rim : rim + rows + 2 * SH] = partial[...]
    window[:, :tall] += before[...]
    window[:, extent - tall :] += after[...]
    out[...] = jnp.zeros_like(out)

    @pl.loop(0, observed.shape[0])
    def _(f):
        p, q = positions[f, 0], positions[f, 1]
        start = lax.rem(strip[0] * rows - EDGE - p + 2 * NX, NX)

        def moved(i):
            return pltpu.roll(rows_from(wrapped.at[i], start, extent), q, 1)

        kappa_row = moved(2)
        probe_re, probe_im = moved(0), moved(1)
        re = probe_re * window[0] - probe_im * window[1]
        im = probe_re * window[1] + probe_im * window[0]
        for _ in range(STEPS):
            re, im = re - kappa_row * laplace(im), im + kappa_row * laplace(re)
        slope = 2.0 * (re * re + im * im - observed[f])
        re, im = slope * re, slope * im
        for _ in range(STEPS):
            re, im = re + laplace(kappa_row * im), im - laplace(kappa_row * re)
        keep = slice(rim, extent - rim)
        out[0] += (probe_re * re + probe_im * im)[keep]
        out[1] += (probe_re * im - probe_im * re)[keep]
        out[2] += (probe_re * probe_re + probe_im * probe_im)[keep]


def frame_gradients(strip, positions, partial, before, after, observed, probe, kappa):
    extent = observed.shape[1]
    smem = pl.BlockSpec(memory_space=pltpu.SMEM)
    vmem = pl.BlockSpec(memory_space=pltpu.VMEM)
    return pl.pallas_call(
        frames_kernel,
        out_shape=jax.ShapeDtypeStruct((3, extent - 2 * (EDGE - SH), NY), jnp.float32),
        in_specs=[smem, smem] + [vmem] * 6,
        out_specs=vmem,
        scratch_shapes=[
            pltpu.VMEM((3, NY // LANES, NX + extent, LANES), jnp.float32),
            pltpu.VMEM((2, extent, NY), jnp.float32),
        ],
        compiler_params=VMEM,
        name="frames",
    )(strip, positions, partial, before, after, observed, probe, kappa)


def update_kernel(shears, field, totals, out):
    depth, rows = field.shape[0], field.shape[2]
    angles = totals.shape[0]
    z0 = pl.program_id(1) * depth
    part = 64 if rows % 64 == 0 else rows

    @pl.loop(0, depth)
    def _(z):
        starts = [SH - shears[a, z0 + z] for a in range(angles)]
        for top in range(0, rows, part):

            def summed(c):
                terms = [totals[a, c, pl.ds(starts[a] + top, part), :] for a in range(angles)]
                return functools.reduce(jnp.add, terms)

            scale = 1.0 / (summed(2) + 1.0)
            for c in range(2):
                at = (z, c, pl.ds(top, part))
                out[at] = field[at] - summed(c) * scale


def update(shears, field, totals):
    slices, _, rows, width = field.shape
    angles, _, tall, _ = totals.shape
    depth = 4
    block = pl.BlockSpec((depth, 2, rows, LANES), lambda i, j: (j, 0, 0, i))
    return pl.pallas_call(
        update_kernel,
        out_shape=jax.ShapeDtypeStruct(field.shape, jnp.float32),
        grid=(width // LANES, slices // depth),
        in_specs=[
            pl.BlockSpec(memory_space=pltpu.SMEM),
            block,
            pl.BlockSpec((angles, 3, tall, LANES), lambda i, j: (0, 0, 0, i)),
        ],
        out_specs=block,
        compiler_params=VMEM,
        name="update",
    )(shears, field, totals)


def per_device(object_field, shears, positions, measured, probe_field, kappa_field):
    strips = lax.axis_size("block")
    rows = object_field.shape[2]
    frames = measured.shape[1]
    tall = EDGE + SH
    strip = lax.axis_index("block").reshape(1)
    all_positions = lax.all_gather(positions[0], "block", axis=0, tiled=True)
    all_shears = lax.all_gather(shears, "angle", axis=0, tiled=True)

    shifted = shift_measured(strips, positions[0], measured[0])
    observed = lax.all_to_all(shifted, "block", 0, 0, tiled=True)
    observed = observed.reshape(strips * frames, rows + 2 * EDGE, NY)

    partial = project(shears, object_field)
    up = [(i, (i + 1) % strips) for i in range(strips)]
    down = [(j, i) for i, j in up]
    before = lax.ppermute(partial[:, rows + 2 * SH - tall :], "block", up)
    after = lax.ppermute(partial[:, :tall], "block", down)

    totals = frame_gradients(
        strip, all_positions, partial, before, after, observed, probe_field, kappa_field[0]
    )
    gathered = lax.all_gather(totals, "angle", axis=0)
    return update(all_shears, object_field, gathered)


def solution(mesh):
    placed = (
        P(None, None, "block", None),
        P("angle", None),
        P("angle", "block", None),
        P("angle", "block", None, None),
        P(),
        P("angle", None, None),
    )
    return jax.shard_map(
        per_device,
        mesh=mesh,
        in_specs=placed,
        out_specs=P(None, None, "block", None),
        check_vma=False,
    )
```

```python
import functools
import jax
import jax.numpy as jnp
from jax import lax
from jax.experimental import pallas as pl
from jax.experimental.pallas import tpu as pltpu
from jax.sharding import PartitionSpec as P

NX = 512
NY = 512
STEPS = 2
SH = 16
EDGE = 24
LANES = 128
MESH = pl.DeviceIdType.MESH
VMEM = pltpu.CompilerParams(vmem_limit_bytes=56 * 1024 * 1024)


def spread(buffer, value, top):
    for j in range(NY // LANES):
        buffer[j, top : top + value.shape[0], :] = value[:, j * LANES : (j + 1) * LANES]


def rows_from(buffer, start, extent):
    parts = [buffer[j, pl.ds(start, extent), :] for j in range(NY // LANES)]
    return jnp.concatenate(parts, axis=1)


def exchange_kernel(
    strips, positions, shears, index_row, observed, field,
    shifted_out, index_out, partial_out, before_out, after_out,
    wrapped, stage, slab0, slab1, partial,
    local_sem, send_sem, recv_sem, index_send, index_recv, rim_send, rim_recv, slab_sem,
):
    me = lax.axis_index("block")
    frames = observed.shape[0]
    slices, _, rows, _ = field.shape
    extent = rows + 2 * EDGE
    tall = EDGE + SH
    blocks = NY // LANES
    depth = slab0.shape[1]

    def fetch(i, slab, slot, j):
        return pltpu.make_async_copy(
            field.at[pl.ds(i * depth, depth), :, :, pl.ds(j * LANES, LANES)],
            slab.at[j, :, :, pl.ds(2 * SH, rows), :],
            slab_sem.at[slot, j],
        )

    for j in range(blocks):
        fetch(0, slab0, 0, j).start()
        fetch(1, slab1, 1, j).start()

    barrier = pltpu.get_barrier_semaphore()
    for k in range(1, strips):
        peer = {"block": lax.rem(me + k, strips)}
        pl.semaphore_signal(barrier, inc=1, device_id=peer, device_id_type=MESH)

    for f in range(frames):
        spread(wrapped.at[f], observed[f].astype(jnp.float32), 0)
        wrapped[f, :, NX:] = wrapped[f, :, :extent]

    def shift(k):
        for f in range(frames):
            p, q = positions[f, 0], positions[f, 1]
            start = lax.rem(lax.rem(me + k, strips) * rows - EDGE - p + 2 * NX, NX)
            stage[k, f] = pltpu.roll(rows_from(wrapped.at[f], start, extent), q, 1)

    def ship(k, slot):
        return pltpu.make_async_remote_copy(
            src_ref=stage.at[k],
            dst_ref=shifted_out.at[slot],
            send_sem=send_sem.at[k],
            recv_sem=recv_sem.at[k],
            device_id={"block": lax.rem(me + k, strips)},
            device_id_type=MESH,
        )

    def ship_index(k, slot):
        return pltpu.make_async_remote_copy(
            src_ref=index_row,
            dst_ref=index_out.at[slot],
            send_sem=index_send.at[k],
            recv_sem=index_recv.at[k],
            device_id={"block": lax.rem(me + k, strips)},
            device_id_type=MESH,
        )

    order = sorted(range(1, strips), key=lambda k: abs(2 * k - strips))
    for n, k in enumerate(order):
        shift(k)
        if n == 0:
            pl.semaphore_wait(barrier, strips - 1)
        ship(k, me).start()
    for k in order:
        ship_index(k, me).start()
    shift(0)
    own = pltpu.make_async_copy(stage.at[0], shifted_out.at[me], local_sem.at[0])
    own_index = pltpu.make_async_copy(index_row, index_out.at[me], local_sem.at[1])
    own.start()
    own_index.start()

    zeros = jnp.zeros((depth, 2, 2 * SH, LANES), jnp.float32)
    for slab in (slab0, slab1):
        for j in range(blocks):
            slab[j, :, :, : 2 * SH] = zeros
            slab[j, :, :, 2 * SH + rows :] = zeros
    partial[...] = jnp.zeros_like(partial)
    rounds = slices // depth

    @pl.loop(0, rounds // 2)
    def _(pair):
        for slot, slab in enumerate((slab0, slab1)):
            i = 2 * pair + slot
            for j in range(blocks):
                fetch(i, slab, slot, j).wait()
            for j in range(blocks):
                for c in range(2):
                    total = partial[c, j]
                    for z in range(depth):
                        at = pl.ds(SH + shears[0, i * depth + z], rows + 2 * SH)
                        total = total + slab[j, z, c, at, :]
                    partial[c, j] = total

            @pl.when(pair < rounds // 2 - 1)
            def _():
                for j in range(blocks):
                    fetch(i + 2, slab, slot, j).start()

    def rim(side):
        step, top, landing = ((1, rows + 2 * SH - tall, before_out), (strips - 1, 0, after_out))[side]
        return pltpu.make_async_remote_copy(
            src_ref=partial.at[:, :, pl.ds(top, tall), :],
            dst_ref=landing,
            send_sem=rim_send.at[side],
            recv_sem=rim_recv.at[side],
            device_id={"block": lax.rem(me + step, strips)},
            device_id_type=MESH,
        )

    rim(0).start()
    rim(1).start()
    whole = pltpu.make_async_copy(partial, partial_out, local_sem.at[2])
    whole.start()
    own.wait()
    own_index.wait()
    whole.wait()
    for side in range(2):
        rim(side).wait()
    for k in order:
        source = lax.rem(me - k + strips, strips)
        ship_index(k, source).wait()
        ship(k, source).wait()


def exchange(strips, positions, shears, index_row, observed, field):
    slices, _, rows, _ = field.shape
    extent = rows + 2 * EDGE
    frames = observed.shape[0]
    blocks = NY // LANES
    depth = 4
    tall = EDGE + SH
    smem = pl.BlockSpec(memory_space=pltpu.SMEM)
    vmem = pl.BlockSpec(memory_space=pltpu.VMEM)
    anyw = pl.BlockSpec(memory_space=pl.ANY)
    f32 = jnp.float32
    slab = pltpu.VMEM((blocks, depth, 2, rows + 4 * SH, LANES), f32)
    dma = pltpu.SemaphoreType.DMA
    return pl.pallas_call(
        functools.partial(exchange_kernel, strips),
        out_shape=[
            jax.ShapeDtypeStruct((strips, frames, extent, NY), f32),
            jax.ShapeDtypeStruct((strips, 8, LANES), jnp.int32),
            jax.ShapeDtypeStruct((2, blocks, rows + 2 * SH, LANES), f32),
            jax.ShapeDtypeStruct((2, blocks, tall, LANES), f32),
            jax.ShapeDtypeStruct((2, blocks, tall, LANES), f32),
        ],
        in_specs=[smem, smem, vmem, vmem, anyw],
        out_specs=[anyw] * 5,
        scratch_shapes=[
            pltpu.VMEM((frames, blocks, NX + extent, LANES), f32),
            pltpu.VMEM((strips, frames, extent, NY), f32),
            slab,
            slab,
            pltpu.VMEM((2, blocks, rows + 2 * SH, LANES), f32),
            dma((3,)),
            dma((strips,)),
            dma((strips,)),
            dma((strips,)),
            dma((strips,)),
            dma((2,)),
            dma((2,)),
            dma((2, blocks)),
        ],
        compiler_params=pltpu.CompilerParams(
            vmem_limit_bytes=56 * 1024 * 1024, collective_id=0, has_side_effects=True
        ),
        name="exchange",
    )(positions, shears, index_row, observed, field)


def gather_kernel(
    held, totals, index_row, probe, out, index_out, weight,
    intensity, table, send_sem, recv_sem, index_send, index_recv, local_sem,
):
    angles = out.shape[0]
    me = lax.axis_index("angle")
    channels, tall = totals.shape[0], totals.shape[1]
    half = tall // 2
    core, x, y = lax.rem(me, 2), lax.rem(me // 2, 2), me // 4
    by_core = me + 1 - 2 * core
    by_x = me + 2 - 4 * x
    by_y = me + 4 - 8 * y
    corner = by_x + 4 - 8 * y

    barrier = pltpu.get_barrier_semaphore()
    for k in range(1, angles):
        peer = {"angle": lax.rem(me + k, angles)}
        pl.semaphore_signal(barrier, inc=1, device_id=peer, device_id_type=MESH)
    pl.semaphore_wait(barrier, angles - 1)

    def index_copy(k, slot):
        return pltpu.make_async_remote_copy(
            src_ref=index_row,
            dst_ref=index_out.at[slot],
            send_sem=index_send.at[k],
            recv_sem=index_recv.at[k],
            device_id={"angle": lax.rem(me + k, angles)},
            device_id_type=MESH,
        )

    def copy(kind, ch, source, owner, rows, target):
        return pltpu.make_async_remote_copy(
            src_ref=source.at[rows],
            dst_ref=out.at[owner, ch, rows],
            send_sem=send_sem.at[kind, ch],
            recv_sem=recv_sem.at[kind, ch],
            device_id={"angle": target},
            device_id_type=MESH,
        )

    every, first, second = pl.ds(0, tall), pl.ds(0, half), pl.ds(half, half)
    plan = (
        (every, by_x, me, by_x),
        (every, by_y, me, by_y),
        (every, by_core, me, by_core),
        (first, by_y, by_x, corner),
        (second, by_x, by_y, corner),
        (every, by_core, by_x, by_x + 1 - 2 * core),
        (every, by_core, by_y, by_y + 1 - 2 * core),
        (first, by_core, corner, corner + 1 - 2 * core),
        (second, by_core, corner, corner + 1 - 2 * core),
    )

    def begin(kind, ch):
        rows, target, owner, _ = plan[kind]
        source = totals.at[ch] if kind < 3 else out.at[owner, ch]
        copy(kind, ch, source, owner, rows, target).start()

    def landed(kind, ch):
        rows, target, _, owner = plan[kind]
        copy(kind, ch, totals.at[ch], owner, rows, target).wait_recv()

    for ch in range(channels):
        for kind in range(3):
            begin(kind, ch)
    for k in range(1, angles):
        index_copy(k, me).start()
    own = pltpu.make_async_copy(totals, out.at[me], local_sem.at[0])
    own_index = pltpu.make_async_copy(index_row, index_out.at[me], local_sem.at[1])
    own.start()
    own_index.start()
    square = probe[0] * probe[0] + probe[1] * probe[1]
    spread(intensity, square, 0)
    spread(intensity, square[:tall], NX)
    own_index.wait()
    for k in range(1, angles):
        index_copy(k, lax.rem(me - k + angles, angles)).wait()
    fill = pltpu.make_async_copy(index_out, table, local_sem.at[2])
    fill.start()
    fill.wait()
    strips = table.shape[1]
    first_row = lax.axis_index("block") * (tall - 2 * SH) - SH

    def weigh(low, high):
        @pl.loop(low, high)
        def _(a):
            total = jnp.zeros((tall, NY), jnp.float32)
            for b in range(strips):
                for f in range(held):
                    p, q = position(table.at[a, b], f)
                    start = lax.rem(first_row - p + 2 * NX, NX)
                    total = total + pltpu.roll(rows_from(intensity, start, tall), q, 1)
            weight[a] = total

    third = angles // 3
    weigh(0, third)
    for ch in range(channels):
        landed(0, ch)
        begin(3, ch)
        begin(5, ch)
        landed(1, ch)
        begin(4, ch)
        begin(6, ch)
    weigh(third, 2 * third)
    for ch in range(channels):
        landed(3, ch)
        begin(7, ch)
        landed(4, ch)
        begin(8, ch)
    weigh(2 * third, angles)
    own.wait()
    for ch in range(channels):
        for kind in (2, 5, 6, 7, 8):
            landed(kind, ch)
        for kind in range(9):
            rows, target, owner, _ = plan[kind]
            source = totals.at[ch] if kind < 3 else out.at[owner, ch]
            copy(kind, ch, source, owner, rows, target).wait_send()


def gather(angles, held, totals, index_row, probe):
    anyw = pl.BlockSpec(memory_space=pl.ANY)
    vmem = pl.BlockSpec(memory_space=pltpu.VMEM)
    dma = pltpu.SemaphoreType.DMA
    channels, tall, _ = totals.shape
    return pl.pallas_call(
        functools.partial(gather_kernel, held),
        out_shape=[
            jax.ShapeDtypeStruct((angles, *totals.shape), jnp.float32),
            jax.ShapeDtypeStruct((angles, *index_row.shape), jnp.int32),
            jax.ShapeDtypeStruct((angles, tall, NY), jnp.float32),
        ],
        in_specs=[anyw, anyw, vmem],
        out_specs=[anyw, anyw, vmem],
        scratch_shapes=[
            pltpu.VMEM((NY // LANES, NX + tall, LANES), jnp.float32),
            pltpu.SMEM((angles, *index_row.shape), jnp.int32),
            dma((9, channels)),
            dma((9, channels)),
            dma((angles,)),
            dma((angles,)),
            dma((3,)),
        ],
        compiler_params=pltpu.CompilerParams(
            vmem_limit_bytes=56 * 1024 * 1024, collective_id=1, has_side_effects=True
        ),
        name="gather",
    )(totals, index_row, probe)


def position(row, f):
    return row[0, LANES // 2 + 2 * f], row[0, LANES // 2 + 2 * f + 1]


def laplace(field):
    rows, columns = field.shape
    return (
        pltpu.roll(field, 1, 0)
        + pltpu.roll(field, rows - 1, 0)
        + pltpu.roll(field, 1, 1)
        + pltpu.roll(field, columns - 1, 1)
        - 4.0 * field
    )


def frames_kernel(strip, positions, partial, before, after, observed, probe, kappa, out, wrapped, window):
    extent = window.shape[1]
    rows = extent - 2 * EDGE
    rim = EDGE - SH
    tall = EDGE + SH
    for i, source in enumerate((probe.at[0], probe.at[1], kappa)):
        spread(wrapped.at[i], source[...], 0)
        spread(wrapped.at[i], source[:extent], NX)
    window[:, :rim] = jnp.zeros((2, rim, NY), jnp.float32)
    window[:, rim + rows + 2 * SH :] = jnp.zeros((2, rim, NY), jnp.float32)
    for j in range(NY // LANES):
        at = slice(j * LANES, (j + 1) * LANES)
        window[:, rim : rim + rows + 2 * SH, at] = partial[:, j]
        window[:, :tall, at] += before[:, j]
        window[:, extent - tall :, at] += after[:, j]
    out[...] = jnp.zeros_like(out)

    strips = positions.shape[0]
    held = observed.shape[0] // strips

    @pl.loop(0, observed.shape[0])
    def _(f):
        p, q = position(positions.at[f // held], lax.rem(f, held))
        start = lax.rem(strip[0] * rows - EDGE - p + 2 * NX, NX)

        def moved(i):
            return pltpu.roll(rows_from(wrapped.at[i], start, extent), q, 1)

        kappa_row = moved(2)
        probe_re, probe_im = moved(0), moved(1)
        re = probe_re * window[0] - probe_im * window[1]
        im = probe_re * window[1] + probe_im * window[0]
        for _ in range(STEPS):
            re, im = re - kappa_row * laplace(im), im + kappa_row * laplace(re)
        slope = 2.0 * (re * re + im * im - observed[f])
        re, im = slope * re, slope * im
        for _ in range(STEPS):
            re, im = re + laplace(kappa_row * im), im - laplace(kappa_row * re)
        keep = slice(rim, extent - rim)
        out[0] += (probe_re * re + probe_im * im)[keep]
        out[1] += (probe_re * im - probe_im * re)[keep]


def frame_gradients(strip, positions, partial, before, after, observed, probe, kappa):
    extent = observed.shape[1]
    smem = pl.BlockSpec(memory_space=pltpu.SMEM)
    vmem = pl.BlockSpec(memory_space=pltpu.VMEM)
    return pl.pallas_call(
        frames_kernel,
        out_shape=jax.ShapeDtypeStruct((2, extent - 2 * (EDGE - SH), NY), jnp.float32),
        in_specs=[smem, smem] + [vmem] * 6,
        out_specs=vmem,
        scratch_shapes=[
            pltpu.VMEM((3, NY // LANES, NX + extent, LANES), jnp.float32),
            pltpu.VMEM((2, extent, NY), jnp.float32),
        ],
        compiler_params=VMEM,
        name="frames",
    )(strip, positions, partial, before, after, observed, probe, kappa)


def update_kernel(shears, field, totals, weight, out):
    depth, rows = field.shape[0], field.shape[2]
    angles = totals.shape[0]
    z0 = pl.program_id(1) * depth
    part = 64 if rows % 64 == 0 else rows

    @pl.loop(0, depth)
    def _(z):
        starts = [SH - shears[a, z0 + z] for a in range(angles)]
        for top in range(0, rows, part):

            def summed(source):
                terms = [source(a)[pl.ds(starts[a] + top, part), :] for a in range(angles)]
                return functools.reduce(jnp.add, terms)

            scale = 1.0 / (summed(lambda a: weight.at[a]) + 1.0)
            for c in range(2):
                at = (z, c, pl.ds(top, part))
                out[at] = field[at] - summed(lambda a: totals.at[a, c]) * scale


def update(shears, field, totals, weight):
    slices, _, rows, width = field.shape
    angles, _, tall, _ = totals.shape
    depth = 4
    block = pl.BlockSpec((depth, 2, rows, LANES), lambda i, j: (j, 0, 0, i))
    return pl.pallas_call(
        update_kernel,
        out_shape=jax.ShapeDtypeStruct(field.shape, jnp.float32),
        grid=(width // LANES, slices // depth),
        in_specs=[
            pl.BlockSpec(memory_space=pltpu.SMEM),
            block,
            pl.BlockSpec((angles, 2, tall, LANES), lambda i, j: (0, 0, 0, i)),
            pl.BlockSpec((angles, tall, LANES), lambda i, j: (0, 0, i)),
        ],
        out_specs=block,
        compiler_params=VMEM,
        name="update",
    )(shears, field, totals, weight)


def per_device(object_field, shears, positions, measured, probe_field, kappa_field):
    strips = lax.axis_size("block")
    rows = object_field.shape[2]
    frames = measured.shape[1]
    strip = lax.axis_index("block").reshape(1)
    angles = lax.axis_size("angle")

    def half_row(values):
        flat = values.reshape(1, -1)
        return jnp.pad(flat, ((0, 7), (0, LANES // 2 - flat.shape[1])))

    index_row = jnp.concatenate([half_row(shears), half_row(positions)], axis=1)
    observed, index_rows, partial, before, after = exchange(
        strips, positions[0], shears, index_row, measured[0], object_field
    )
    observed = observed.reshape(strips * frames, rows + 2 * EDGE, NY)
    totals = frame_gradients(
        strip, index_rows, partial, before, after, observed, probe_field, kappa_field[0]
    )
    slices = object_field.shape[0]
    if angles == 8:
        gathered, table, weight = gather(angles, frames, totals, index_rows, probe_field)
        all_shears = table[:, 0, 0, :slices]
    else:
        gathered = lax.all_gather(totals, "angle", axis=0)
        all_shears = lax.all_gather(shears, "angle", axis=0, tiled=True)
        weight = weights_here(strip, index_rows, probe_field, rows)
        weight = lax.all_gather(weight, "angle", axis=0)
    return update(all_shears, object_field, gathered, weight)


def weights_here(strip, index_rows, probe_field, rows):
    intensity = probe_field[0] * probe_field[0] + probe_field[1] * probe_field[1]
    offsets = index_rows[:, 0, LANES // 2 : LANES // 2 + 2]
    total = 0.0
    for b in range(index_rows.shape[0]):
        top = SH - strip[0] * rows
        moved = jnp.roll(intensity, (offsets[b, 0] + top, offsets[b, 1]), axis=(0, 1))
        total = total + moved[: rows + 2 * SH]
    return total


def solution(mesh):
    placed = (
        P(None, None, "block", None),
        P("angle", None),
        P("angle", "block", None),
        P("angle", "block", None, None),
        P(),
        P("angle", None, None),
    )
    return jax.shard_map(
        per_device,
        mesh=mesh,
        in_specs=placed,
        out_specs=P(None, None, "block", None),
        check_vma=False,
    )
```
